32 devices in a mesh: dp: 16 (over z, x, core), group: 2 (over y).
Axes of the slice: x: 2, y: 2, z: 4, core: 2. Of those that a mesh axis runs over, the one named last changes fastest.
Arguments:
- tokens: bfloat16 [8192, 896], P(('dp', 'group')), may hold values from -6 to 6
- cotangent: bfloat16 [8192, 896], P(('dp', 'group')), may hold values from -6 to 6
- lengths: int32 [32, 4], P(('dp', 'group')), may hold values from 0 to 256, as said below
- qkv_weight: float32 [896, 1152], P('group'), may hold values from -0.1875 to 0.1875
- out_weight: float32 [896, 896], P('group'), may hold values from -2 to 2
- expand_weight: float32 [896, 9728], P('group'), may hold values from -0.1875 to 0.1875
- down_weight: float32 [4864, 896], P('group'), may hold values from -0.15625 to 0.15625
- norm_gains: float32 [1792], P('group'), may hold values from 0.5 to 1.5
- qkv_biases: float32 [1152], P('group'), may hold values from -1.5 to 1.5
- qkv_first: float32 [896, 1152], P('group'), may hold values from -80 to 80
- out_first: float32 [896, 896], P('group'), may hold values from -10 to 10
- expand_first: float32 [896, 9728], P('group'), may hold values from -24 to 24
- down_first: float32 [4864, 896], P('group'), may hold values from -32 to 32
- gains_first: float32 [1792], P('group'), may hold values from -80 to 80
- biases_first: float32 [1152], P('group'), may hold values from -80 to 80
- qkv_second: float32 [896, 1152], P('group'), may hold values from 18.432 to 73.728
- out_second: float32 [896, 896], P('group'), may hold values from 0.18432 to 0.73728
- expand_second: float32 [896, 9728], P('group'), may hold values from 1.31072 to 5.24288
- down_second: float32 [4864, 896], P('group'), may hold values from 2.94912 to 11.79648
- gains_second: float32 [1792], P('group'), may hold values from 18.432 to 73.728
- biases_second: float32 [1152], P('group'), may hold values from 18.432 to 73.728
Outputs:
- output: bfloat16 [8192, 896], P(('dp', 'group'))
- token_grad: bfloat16 [8192, 896], P(('dp', 'group'))
- qkv_gradient: bfloat16 [896, 1152], P('group')
- out_gradient: bfloat16 [896, 896], P('group')
- expand_gradient: bfloat16 [896, 9728], P('group')
- down_gradient: bfloat16 [4864, 896], P('group')
- gains_gradient: bfloat16 [1792], P('group')
- biases_gradient: bfloat16 [1152], P('group')
- qkv_updated: float32 [896, 1152], P('group')
- out_updated: float32 [896, 896], P('group')
- expand_updated: float32 [896, 9728], P('group')
- down_updated: float32 [4864, 896], P('group')
- gains_updated: float32 [1792], P('group')
- biases_updated: float32 [1152], P('group')
- qkv_momentum: float32 [896, 1152], P('group')
- out_momentum: float32 [896, 896], P('group')
- expand_momentum: float32 [896, 9728], P('group')
- down_momentum: float32 [4864, 896], P('group')
- gains_momentum: float32 [1792], P('group')
- biases_momentum: float32 [1152], P('group')
- qkv_variance: float32 [896, 1152], P('group')
- out_variance: float32 [896, 896], P('group')
- expand_variance: float32 [896, 9728], P('group')
- down_variance: float32 [4864, 896], P('group')
- gains_variance: float32 [1792], P('group')
- biases_variance: float32 [1152], P('group')
The draws below stay inside these ranges and needn't reach their ends.
Inputs may be any that keep to these rules, and one draw needn't show every extreme that they name: Row r lists the lengths of the sequences packed from the first of device r's 256 rows; a row's lengths sum to 128 or more and to 256 at most, and a length may be 0; in every draw one device holds a single sequence of 256 rows.
All inputs are finite; a program needn't handle non-finite values.
Results may differ from the reference program's by a relative error of at most 0.014.
The reference program's roundings to bfloat16 on the way count: a program that leaves them out, or rounds other values in their place, can miss the bound.
Values may be sent and summed in bfloat16 or wider, within the bound.
A program may use at most 512 MiB of HBM per device.

```python
import math
import jax
import jax.numpy as jnp
from jax import lax

D = 896
HEADS = 14
KV_HEADS = 2
HEAD_DIM = 64
FF = 4864
TOK_DEV = 256
SLOTS = 4
STEP = 10
TOKENS = 8192
QKV_WIDTH = 1152
N_DP = 16
N_GROUP = 2


def draw_lengths(key, part):
    key = jax.random.fold_in(key, 11)
    buffers = TOKENS // TOK_DEV
    subkeys = jax.random.split(key, 3)
    totals = jax.random.randint(subkeys[0], (buffers, 1), TOK_DEV // 2, TOK_DEV + 1)
    cut_points = jax.random.randint(subkeys[1], (buffers, SLOTS - 1), 0, totals + 1)
    cut_points = jnp.sort(cut_points, axis=1)
    boundary = jnp.concatenate([jnp.zeros((buffers, 1), jnp.int32), cut_points.astype(jnp.int32), totals.astype(jnp.int32)], axis=1)
    spans = boundary[:, 1:] - boundary[:, :-1]
    chosen = jax.random.randint(subkeys[2], (), 0, buffers)
    full_row = jnp.zeros((SLOTS,), jnp.int32).at[0].set(TOK_DEV)
    row_ids = jnp.arange(buffers)[:, None]
    return jnp.where(row_ids == chosen, full_row[None, :], spans).astype(jnp.int32)


def raised(array, own_key, source, target, parts, factor):
    def block_of(axis_at):
        return (jnp.arange(array.shape[axis_at]) // (array.shape[axis_at] // parts)).reshape((-1,) + (1,) * (array.ndim - 1 - axis_at))

    first = jax.random.permutation(own_key, parts)[block_of(target)]
    far = (block_of(target) + parts // 2) % parts
    return jnp.where((block_of(source) == first) | (block_of(source) == far), factor * array, array)


def block_scale(stream_key, shape, cuts, smallest, top_value):
    def one(dim, shards_of):
        draws = jax.random.uniform(jax.random.fold_in(jax.random.fold_in(stream_key, 6), dim), (shards_of,), jnp.float32, smallest / len(cuts), top_value / len(cuts))
        return jnp.repeat(jnp.exp(draws), shape[dim] // shards_of).reshape((-1,) + (1,) * (len(shape) - dim - 1))

    loudness = one(*cuts[0])
    for cut in cuts[1:]:
        loudness = loudness * one(*cut)
    return loudness


def noise(key, extent, deviation, bound, pieces=(), kind=jnp.bfloat16):
    level = block_scale(key, extent, pieces, -0.22, 0.18) if pieces else 1.0
    entries = jax.random.normal(key, extent, jnp.float32) * deviation * level
    return jnp.minimum(jnp.maximum(entries, -bound), bound).astype(kind)


def noise_with(stream_key, shape, spread, bound, pieces, heavy, held_as=jnp.bfloat16):
    values = spread * jax.random.normal(stream_key, shape, jnp.float32)
    if pieces:
        values = values * block_scale(stream_key, shape, pieces, -0.22, 0.18)
    return jnp.clip(raised(values, jax.random.fold_in(stream_key, 3), *heavy), -bound, bound).astype(held_as)


def setup_inputs(seed: int = 0) -> dict:
    streams_of = jax.random.split(jax.random.key(seed), 22)
    tokens = noise_with(streams_of[0], (TOKENS, D), 1.0, 6.0, ((0, 32),), (0, 1, 32, 2.75))
    cotangent = noise(streams_of[1], (TOKENS, D), 1.0, 6.0, ((0, 32),))
    lengths = draw_lengths(jax.random.fold_in(streams_of[21], 71), 0)
    qkv_weight = noise(streams_of[3], (D, QKV_WIDTH), D ** -0.5, 0.1875, ((0, 2),), jnp.float32)
    out_weight = noise(streams_of[4], (D, D), (max(D // 96, 1)) ** -0.5, 2.0, ((0, 2),), jnp.float32)
    expand_weight = noise(streams_of[5], (D, 2 * FF), D ** -0.5, 0.1875, ((0, 2),), jnp.float32)
    down_weight = noise(streams_of[6], (FF, D), (FF // 3) ** -0.5, 0.15625, ((0, 2),), jnp.float32)
    norm_gains = jnp.clip(1.0 + 0.1 * jax.random.normal(streams_of[7], (2 * D,), jnp.float32), 0.5, 1.5)
    qkv_biases = noise(streams_of[8], (QKV_WIDTH,), 0.3, 1.5, ((0, 2),), jnp.float32)
    qkv_first = noise(streams_of[9], (D, QKV_WIDTH), (0.16 * TOKENS ** 0.5), 80.0, ((0, 2),), jnp.float32)
    out_first = noise(streams_of[10], (D, D), (0.017 * TOKENS ** 0.5), 10.0, ((0, 2),), jnp.float32)
    expand_first = noise(streams_of[11], (D, 2 * FF), (0.044 * TOKENS ** 0.5), 24.0, ((0, 2),), jnp.float32)
    down_first = noise(streams_of[12], (FF, D), (0.067 * TOKENS ** 0.5), 32.0, ((0, 2),), jnp.float32)
    gains_first = noise(streams_of[13], (2 * D,), (0.16 * TOKENS ** 0.5), 80.0, ((0, 2),), jnp.float32)
    biases_first = noise(streams_of[14], (QKV_WIDTH,), (0.16 * TOKENS ** 0.5), 80.0, ((0, 2),), jnp.float32)
    qkv_second = jnp.clip(jnp.exp(math.log(73.728) - 1.3862944 * jax.random.uniform(streams_of[15], (D, QKV_WIDTH), jnp.float32) ** block_scale(streams_of[15], (D, QKV_WIDTH), ((0, 2),), -0.2, 0.2)), 18.432, 73.728)
    out_second = jnp.clip(jnp.exp(math.log(0.73728) - 1.3862944 * jax.random.uniform(streams_of[16], (D, D), jnp.float32) ** block_scale(streams_of[16], (D, D), ((0, 2),), -0.2, 0.2)), 0.18432, 0.73728)
    expand_second = jnp.clip(jnp.exp(math.log(5.24288) - 1.3862944 * jax.random.uniform(streams_of[17], (D, 2 * FF), jnp.float32) ** block_scale(streams_of[17], (D, 2 * FF), ((0, 2),), -0.2, 0.2)), 1.31072, 5.24288)
    down_second = jnp.clip(jnp.exp(math.log(11.79648) - 1.3862944 * jax.random.uniform(streams_of[18], (FF, D), jnp.float32) ** block_scale(streams_of[18], (FF, D), ((0, 2),), -0.2, 0.2)), 2.94912, 11.79648)
    gains_second = jnp.clip(jnp.exp(math.log(73.728) - 1.3862944 * jax.random.uniform(streams_of[19], (2 * D,), jnp.float32) ** block_scale(streams_of[19], (2 * D,), ((0, 2),), -0.2, 0.2)), 18.432, 73.728)
    biases_second = jnp.clip(jnp.exp(math.log(73.728) - 1.3862944 * jax.random.uniform(streams_of[20], (QKV_WIDTH,), jnp.float32) ** block_scale(streams_of[20], (QKV_WIDTH,), ((0, 2),), -0.2, 0.2)), 18.432, 73.728)
    return {"tokens": tokens, "cotangent": cotangent, "lengths": lengths, "qkv_weight": qkv_weight, "out_weight": out_weight, "expand_weight": expand_weight, "down_weight": down_weight, "norm_gains": norm_gains, "qkv_biases": qkv_biases, "qkv_first": qkv_first, "out_first": out_first, "expand_first": expand_first, "down_first": down_first, "gains_first": gains_first, "biases_first": biases_first, "qkv_second": qkv_second, "out_second": out_second, "expand_second": expand_second, "down_second": down_second, "gains_second": gains_second, "biases_second": biases_second}


@jax.custom_vjp
def low(v):
    return lax.optimization_barrier(v.astype(jnp.bfloat16)).astype(jnp.float32)

@jax.custom_vjp
def low_back(v):
    return v

def low_keep(v):
    return (low(v), None)

def low_pass(kept, grad):
    return (grad,)

def back_keep(v):
    return (v, None)

def back_low(kept, grad):
    return (low(grad),)
low.defvjp(low_keep, low_pass)
low_back.defvjp(back_keep, back_low)
EPS_NORM = 1e-06
THETA = 1000000.0
MASKED = -1e+30
BETA_ONE = 0.9
BETA_TWO = 0.999
EPS_ADAM = 1e-08
DECAY = 0.1
RATE_MATRIX = 0.08
RATE_OUT = 0.8
RATE_VECTOR = 0.6

def precise_dot(left_in, right_in):
    return jnp.dot(left_in, right_in, precision=lax.Precision.HIGHEST, preferred_element_type=jnp.float32)

def layout(length_row, row_count):
    seq_ends = jnp.cumsum(length_row).astype(jnp.int32)
    row_ids = jnp.arange(row_count, dtype=jnp.int32)
    segment = lax.optimization_barrier(jnp.sum((row_ids[:, None] >= seq_ends[None, :]).astype(jnp.int32), axis=1)).astype(jnp.int32)
    seq_starts = jnp.concatenate([jnp.zeros((1,), jnp.int32), seq_ends]).astype(jnp.int32)
    slot_ids = jnp.arange(seq_starts.shape[0], dtype=jnp.int32)
    seq_begin = lax.optimization_barrier(jnp.sum(jnp.where(segment[:, None] == slot_ids[None, :], seq_starts[None, :], 0), axis=1)).astype(jnp.int32)
    return (segment, (row_ids - seq_begin).astype(jnp.int32), row_ids < seq_ends[-1])

def rope_tables(position, head_size):
    half_dim = head_size // 2
    frequency = THETA ** (-(jnp.arange(half_dim, dtype=jnp.float32) * (2.0 / head_size)))
    angles = position.astype(jnp.float32)[:, None] * frequency[None, :]
    return (jnp.cos(angles), jnp.sin(angles))

def rotate(values, cosine, sine_table):
    half_dim = values.shape[-1] // 2
    first_half = values[..., :half_dim]
    second_half = values[..., half_dim:]
    cos_b = cosine[:, None, :]
    sin_b = sine_table[:, None, :]
    return jnp.concatenate([first_half * cos_b - second_half * sin_b, second_half * cos_b + first_half * sin_b], axis=-1)

def normalize(values, gain_row):
    scaling = lax.rsqrt(lax.optimization_barrier(jnp.mean(values * values, axis=-1, keepdims=True)) + EPS_NORM)
    return values * scaling * gain_row

def swiglu(expanded):
    half_cols = expanded.shape[1] // 2
    return jax.nn.silu(expanded[:, :half_cols]) * expanded[:, half_cols:]

def forward(weights, inputs, segment, position):
    w_qkv, w_out, w_expand, w_down, gains_all, biases_all = weights
    row_count = inputs.shape[0]
    model_width = inputs.shape[1]
    kv_width = KV_HEADS * HEAD_DIM
    repeat = HEADS // KV_HEADS
    cosine, sine_table = rope_tables(position, HEAD_DIM)
    normed = low(normalize(inputs, gains_all[:model_width]))
    projected = low_back(precise_dot(normed, w_qkv) + biases_all)
    queries = rotate(projected[:, :model_width].reshape(row_count, HEADS, HEAD_DIM), cosine, sine_table)
    keys_rot = rotate(projected[:, model_width:model_width + kv_width].reshape(row_count, KV_HEADS, HEAD_DIM), cosine, sine_table)
    queries_low = low(queries).reshape(row_count, KV_HEADS, repeat, HEAD_DIM)
    keys_low = low(keys_rot)
    values_low = low(projected[:, model_width + kv_width:].reshape(row_count, KV_HEADS, HEAD_DIM))
    raw_scores = jnp.einsum('qgrd,kgd->grqk', queries_low, keys_low, precision=lax.Precision.HIGHEST) * HEAD_DIM ** (-0.5)
    row_index = jnp.arange(row_count, dtype=jnp.int32)
    allowed = (segment[:, None] == segment[None, :]) & (row_index[None, :] <= row_index[:, None])
    scores = low_back(jnp.where(allowed[None, None], raw_scores, MASKED))
    soft_weights = low(jax.nn.softmax(scores, axis=-1))
    attended = jnp.einsum('grqk,kgd->qgrd', soft_weights, values_low, precision=lax.Precision.HIGHEST).reshape(row_count, model_width)
    attended = low(low_back(attended))
    hidden = inputs + low_back(precise_dot(attended, w_out))
    normed_two = low(normalize(hidden, gains_all[model_width:]))
    expanded = low_back(precise_dot(normed_two, w_expand))
    activated = low(swiglu(expanded))
    return hidden + low_back(precise_dot(activated, w_down))

def adamw(master, first_old, second_old, gradient, step_rate, decay_rate):
    first_new = BETA_ONE * first_old + (1.0 - BETA_ONE) * gradient
    second_new = BETA_TWO * second_old + (1.0 - BETA_TWO) * gradient * gradient
    direction = first_new / (1.0 - BETA_ONE ** STEP) / (jnp.sqrt(second_new / (1.0 - BETA_TWO ** STEP)) + EPS_ADAM)
    return (master - step_rate * (direction + decay_rate * master), first_new, second_new)

def reference(tokens, cotangent, lengths, qkv_weight, out_weight, expand_weight, down_weight, norm_gains, qkv_biases, qkv_first, out_first, expand_first, down_first, gains_first, biases_first, qkv_second, out_second, expand_second, down_second, gains_second, biases_second):
    masters = (qkv_weight, out_weight, expand_weight, down_weight, norm_gains, qkv_biases)
    firsts = (qkv_first, out_first, expand_first, down_first, gains_first, biases_first)
    seconds = (qkv_second, out_second, expand_second, down_second, gains_second, biases_second)
    rounded = tuple((low(master) for master in masters))
    buffers = N_DP * N_GROUP
    token_rows = tokens.astype(jnp.float32).reshape(buffers, TOK_DEV, D)
    back_rows = cotangent.astype(jnp.float32).reshape(buffers, TOK_DEV, D)
    zero_grads = tuple((jnp.zeros(master.shape, jnp.float32) for master in masters))

    def visit_device(running, item_now):
        rows_one, back_one, length_row = item_now
        segment, position, valid_flag = layout(length_row, TOK_DEV)
        valid_rows = valid_flag.astype(jnp.float32)[:, None]
        result, pullback = jax.vjp(lambda weights, inputs: forward(weights, inputs, segment, position), rounded, rows_one)
        gradients, input_grad = pullback(back_one * valid_rows)
        running = tuple((total_now + piece_now for total_now, piece_now in zip(running, gradients)))
        return (running, ((result * valid_rows).astype(jnp.bfloat16), (input_grad * valid_rows).astype(jnp.bfloat16)))
    gradients, (outputs, input_grads) = lax.scan(visit_device, zero_grads, (token_rows, back_rows, lengths))
    rates = (RATE_MATRIX, RATE_OUT, RATE_MATRIX, RATE_MATRIX, RATE_VECTOR, RATE_VECTOR)
    decays = (DECAY, DECAY, DECAY, DECAY, 0.0, 0.0)
    grads_low, updated, momenta, variances = ([], [], [], [])
    for master, first_old, second_old, gradient, step_rate, decay_rate in zip(masters, firsts, seconds, gradients, rates, decays):
        weight_new, first_new, second_new = adamw(master, first_old, second_old, gradient, step_rate, decay_rate)
        grads_low.append(gradient.astype(jnp.bfloat16))
        updated.append(weight_new)
        momenta.append(first_new)
        variances.append(second_new)
    return (outputs.reshape(TOKENS, D), input_grads.reshape(TOKENS, D), grads_low[0], grads_low[1], grads_low[2], grads_low[3], grads_low[4], grads_low[5], updated[0], updated[1], updated[2], updated[3], updated[4], updated[5], momenta[0], momenta[1], momenta[2], momenta[3], momenta[4], momenta[5], variances[0], variances[1], variances[2], variances[3], variances[4], variances[5])
```

```python
import jax
import jax.numpy as jnp
from jax import lax
from jax.sharding import PartitionSpec as P

D = 896
HEADS = 14
KV_HEADS = 2
HEAD_DIM = 64
STEP = 10


EPS_NORM = 1e-06
THETA = 1000000.0
MASKED = -1e30
BETA_ONE = 0.9
BETA_TWO = 0.999
EPS_ADAM = 1e-08
DECAY = 0.1
RATE_MATRIX = 0.08
RATE_OUT = 0.8
RATE_VECTOR = 0.6


def layout(length_row, row_count):
    seq_ends = jnp.cumsum(length_row)
    row_ids = jnp.arange(row_count, dtype=jnp.int32)
    segment = jnp.sum((row_ids[:, None] >= seq_ends[None, :]).astype(jnp.int32), axis=1)
    seq_starts = jnp.concatenate([jnp.zeros((1,), jnp.int32), seq_ends])
    slot_ids = jnp.arange(seq_starts.shape[0], dtype=jnp.int32)
    seq_begin = jnp.sum(
        jnp.where(segment[:, None] == slot_ids[None, :], seq_starts[None, :], 0), axis=1
    )
    return (segment, row_ids - seq_begin, row_ids < seq_ends[-1])


def rope_tables(position, head_size):
    half_dim = head_size // 2
    frequency = THETA ** (-(jnp.arange(half_dim, dtype=jnp.float32) * (2.0 / head_size)))
    angles = position.astype(jnp.float32)[:, None] * frequency[None, :]
    return (jnp.cos(angles), jnp.sin(angles))


def rotate(values, cosine, sine_table):
    half_dim = values.shape[-1] // 2
    first_half = values[..., :half_dim]
    second_half = values[..., half_dim:]
    cos_b = cosine[:, None, :]
    sin_b = sine_table[:, None, :]
    return jnp.concatenate(
        [first_half * cos_b - second_half * sin_b, second_half * cos_b + first_half * sin_b],
        axis=-1,
    )


def normalize(values, gain_row):
    scaling = lax.rsqrt(jnp.mean(values * values, axis=-1, keepdims=True) + EPS_NORM)
    return values * scaling * gain_row


def adamw(master, first_old, second_old, gradient, step_rate, decay_rate):
    first_new = BETA_ONE * first_old + (1.0 - BETA_ONE) * gradient
    second_new = BETA_TWO * second_old + (1.0 - BETA_TWO) * gradient * gradient
    direction = (
        first_new
        / (1.0 - BETA_ONE**STEP)
        / (jnp.sqrt(second_new / (1.0 - BETA_TWO**STEP)) + EPS_ADAM)
    )
    return (master - step_rate * (direction + decay_rate * master), first_new, second_new)


def local(
    tokens,
    cotangent,
    lengths,
    qkv_weight,
    out_weight,
    expand_weight,
    down_weight,
    norm_gains,
    qkv_biases,
    qkv_first,
    out_first,
    expand_first,
    down_first,
    gains_first,
    biases_first,
    qkv_second,
    out_second,
    expand_second,
    down_second,
    gains_second,
    biases_second,
):
    masters = (qkv_weight, out_weight, expand_weight, down_weight, norm_gains, qkv_biases)
    firsts = (qkv_first, out_first, expand_first, down_first, gains_first, biases_first)
    seconds = (qkv_second, out_second, expand_second, down_second, gains_second, biases_second)
    groups = lax.axis_size("group")
    data_size = lax.axis_size("dp")
    member = lax.axis_index("dp")
    row_parts = data_size // 2
    col_part, row_part = member // row_parts, member % row_parts
    attn_cols = (qkv_weight.shape[1] + out_weight.shape[1]) // 2
    qkv_tail = qkv_weight.shape[1] - attn_cols
    shard_rows = out_weight.shape[0]
    piece_rows = shard_rows // row_parts
    both = ("dp", "group")

    def own_piece(left, right):
        start = row_part * piece_rows
        return jnp.where(
            col_part == 0,
            lax.dynamic_slice_in_dim(left, start, piece_rows, 0),
            lax.dynamic_slice_in_dim(right, start, piece_rows, 0),
        ).astype(jnp.bfloat16)

    def deal(values):
        rows = values.shape[0]
        split = values.reshape(rows, groups, row_parts, piece_rows)
        return jnp.swapaxes(split, 1, 2).reshape(rows, D)

    def undeal(values):
        rows = values.shape[0]
        split = values.reshape(rows, row_parts, groups, piece_rows)
        return jnp.swapaxes(split, 1, 2).reshape(rows, D)

    def scatter_sum(partial):
        return lax.psum_scatter(partial, both, scatter_dimension=0, tiled=True)

    attn_piece = own_piece(
        qkv_weight[:, :attn_cols], jnp.concatenate([qkv_weight[:, attn_cols:], out_weight], axis=1)
    )
    w_attn = lax.all_gather(attn_piece, both, axis=0, tiled=True)
    half_ff = expand_weight.shape[1] // 2
    expand_piece = own_piece(expand_weight[:, :half_ff], expand_weight[:, half_ff:])
    w_expand = lax.all_gather(expand_piece, both, axis=0, tiled=True)
    down_rows = down_weight.shape[0] // data_size
    down_piece = lax.dynamic_slice_in_dim(down_weight, member * down_rows, down_rows, 0)
    w_down = lax.all_gather(
        down_piece.astype(jnp.bfloat16), ("group", "dp"), axis=0, tiled=True
    )
    w_qkv = jnp.concatenate([w_attn[:D], w_attn[D:, :qkv_tail]], axis=1)
    w_out = w_attn[D:, qkv_tail:]
    w_gate, w_up = w_expand[:D], w_expand[D:]
    vectors = lax.all_gather(
        jnp.concatenate([norm_gains, qkv_biases]).astype(jnp.bfloat16), "group", axis=0
    )
    own_gains = norm_gains.shape[0]
    gains_low = vectors[:, :own_gains].reshape(-1)
    biases_low = vectors[:, own_gains:].reshape(-1)
    row_count = tokens.shape[0]
    block_rows = min(512, row_count)
    kv_width = KV_HEADS * HEAD_DIM
    repeat = HEADS // KV_HEADS
    scaling = HEAD_DIM ** (-0.5)
    segment, position, valid_flag = layout(lengths[0], row_count)
    valid_rows = valid_flag.astype(jnp.float32)[:, None]
    cosine, sine_table = rope_tables(position, HEAD_DIM)
    inputs = tokens.astype(jnp.float32)
    gains_all = gains_low.astype(jnp.float32)
    normed, norm_back_one = jax.vjp(normalize, inputs, gains_all[:D])
    normed_low = normed.astype(jnp.bfloat16)
    normed_deal = deal(normed_low)
    projected = jnp.dot(normed_deal, w_qkv, preferred_element_type=jnp.float32) + biases_low.astype(
        jnp.float32
    )
    queries = projected[:, :D].reshape(row_count, HEADS, HEAD_DIM)
    keys_pre = projected[:, D : D + kv_width].reshape(row_count, KV_HEADS, HEAD_DIM)
    values_low = (
        projected[:, D + kv_width :].reshape(row_count, KV_HEADS, HEAD_DIM).astype(jnp.bfloat16)
    )
    (queries_rot, keys_rot), rope_back = jax.vjp(
        lambda query_in, key_in: (
            rotate(query_in, cosine, sine_table),
            rotate(key_in, cosine, sine_table),
        ),
        queries,
        keys_pre,
    )
    queries_low = queries_rot.astype(jnp.bfloat16).reshape(row_count, KV_HEADS, repeat, HEAD_DIM)
    keys_low = keys_rot.astype(jnp.bfloat16)
    key_index = jnp.arange(row_count, dtype=jnp.int32)

    def block_scores(offset):
        raw_scores = (
            jnp.einsum("qgrd,kgd->grqk", queries_low, keys_low, preferred_element_type=jnp.float32)
            * scaling
        )
        allowed = (segment[offset : offset + block_rows, None] == segment[None, :]) & (
            key_index[None, :] <= key_index[:, None]
        )
        return jnp.where(allowed[None, None], raw_scores, MASKED)

    offsets = list(range(0, row_count, block_rows))
    attended_parts, log_parts = ([], [])
    for offset in offsets:
        scores = block_scores(offset)
        highest = jnp.max(scores, axis=-1, keepdims=True)
        exponent = jnp.exp(scores - highest)
        totals = jnp.sum(exponent, axis=-1, keepdims=True)
        soft_low = (exponent / totals).astype(jnp.bfloat16)
        attended_parts.append(
            jnp.einsum("grqk,kgd->qgrd", soft_low, values_low, preferred_element_type=jnp.float32)
        )
        log_parts.append(highest + jnp.log(totals))
    attended = attended_parts[0].reshape(row_count, D).astype(jnp.bfloat16)
    attended_deal = deal(attended)
    hidden = inputs + jnp.dot(attended_deal, w_out, preferred_element_type=jnp.float32)
    normed_two, norm_back_two = jax.vjp(normalize, hidden, gains_all[D:])
    normed_two_low = normed_two.astype(jnp.bfloat16)
    two_deal = deal(normed_two_low)
    gate = jnp.dot(two_deal, w_gate, preferred_element_type=jnp.float32)
    up = jnp.dot(two_deal, w_up, preferred_element_type=jnp.float32)
    activated, gate_back = jax.vjp(lambda g, u: jax.nn.silu(g) * u, gate, up)
    activated_low = activated.astype(jnp.bfloat16)
    result = hidden + jnp.dot(activated_low, w_down, preferred_element_type=jnp.float32)
    output = (result * valid_rows).astype(jnp.bfloat16)
    upstream = cotangent.astype(jnp.float32) * valid_rows
    upstream_low = upstream.astype(jnp.bfloat16)
    grad_down = jnp.einsum(
        "nf,nd->fd", activated_low, upstream_low, preferred_element_type=jnp.float32
    ).astype(jnp.bfloat16)
    piece_down = lax.psum_scatter(grad_down, ("group", "dp"), scatter_dimension=0, tiled=True)
    back_act = jnp.einsum("nd,fd->nf", upstream_low, w_down, preferred_element_type=jnp.float32)
    back_gate, back_up = (part.astype(jnp.bfloat16) for part in gate_back(back_act))
    grad_expand = jnp.concatenate(
        [
            jnp.einsum("nd,nf->df", two_deal, part, preferred_element_type=jnp.float32).astype(
                jnp.bfloat16
            )
            for part in (back_gate, back_up)
        ],
        axis=0,
    )
    piece_expand = scatter_sum(grad_expand)
    back_normed_two = undeal(
        jnp.einsum("nf,df->nd", back_gate, w_gate, preferred_element_type=jnp.float32)
        + jnp.einsum("nf,df->nd", back_up, w_up, preferred_element_type=jnp.float32)
    )
    back_hidden_part, grad_gain_two = norm_back_two(back_normed_two)
    back_hidden = upstream + back_hidden_part
    back_branch = back_hidden.astype(jnp.bfloat16)
    grad_out = jnp.einsum(
        "nd,ne->de", attended_deal, back_branch, preferred_element_type=jnp.float32
    ).astype(jnp.bfloat16)
    back_attended = jnp.einsum("ne,de->nd", back_branch, w_out, preferred_element_type=jnp.float32)
    back_attended = undeal(back_attended.astype(jnp.bfloat16)).reshape(
        row_count, KV_HEADS, repeat, HEAD_DIM
    )
    query_grads = []
    key_grad = jnp.zeros((row_count, KV_HEADS, HEAD_DIM), jnp.float32)
    value_grad = jnp.zeros((row_count, KV_HEADS, HEAD_DIM), jnp.float32)
    for position_block, offset in enumerate(offsets):
        scores = block_scores(offset)
        soft_weights = jnp.exp(scores - log_parts[position_block])
        back_soft = jnp.einsum(
            "qgrd,kgd->grqk", back_attended, values_low, preferred_element_type=jnp.float32
        )
        inner_sum = jnp.sum(soft_weights * back_soft, axis=-1, keepdims=True)
        back_scores = (soft_weights * (back_soft - inner_sum)).astype(jnp.bfloat16)
        query_grads.append(
            jnp.einsum("grqk,kgd->qgrd", back_scores, keys_low, preferred_element_type=jnp.float32)
            * scaling
        )
        key_grad = (
            jnp.einsum(
                "grqk,qgrd->kgd", back_scores, queries_low, preferred_element_type=jnp.float32
            )
            * scaling
        )
        value_grad = jnp.einsum(
            "grqk,qgrd->kgd",
            soft_weights.astype(jnp.bfloat16),
            back_attended,
            preferred_element_type=jnp.float32,
        )
    back_queries = query_grads[0].reshape(row_count, HEADS, HEAD_DIM)
    back_query_pre, back_key_pre = rope_back((back_queries, key_grad))
    back_projected = jnp.concatenate(
        [
            back_query_pre.reshape(row_count, D),
            back_key_pre.reshape(row_count, kv_width),
            value_grad.reshape(row_count, kv_width),
        ],
        axis=1,
    ).astype(jnp.bfloat16)
    grad_biases = jnp.sum(back_projected, axis=0, dtype=jnp.float32)
    grad_qkv = jnp.einsum(
        "nd,ne->de", normed_deal, back_projected, preferred_element_type=jnp.float32
    ).astype(jnp.bfloat16)
    grad_attn = jnp.concatenate(
        [
            grad_qkv[:, :attn_cols],
            jnp.concatenate([grad_qkv[:, attn_cols:], grad_out], axis=1),
        ],
        axis=0,
    )
    piece_attn = scatter_sum(grad_attn)
    back_normed = undeal(
        jnp.einsum("ne,de->nd", back_projected, w_qkv, preferred_element_type=jnp.float32)
    )
    back_inputs, grad_gain_one = norm_back_one(back_normed)
    token_grad = (back_hidden + back_inputs).astype(jnp.bfloat16)
    small = jnp.concatenate(
        [
            jnp.concatenate([grad_gain_one, grad_gain_two]).reshape(groups, -1),
            grad_biases.reshape(groups, -1),
        ],
        axis=1,
    )
    small = lax.psum(small, both)[lax.axis_index("group")]
    own_down = lax.all_gather(piece_down, "dp", axis=0, tiled=True)
    own_expand = lax.all_gather(piece_expand, "dp", axis=0, tiled=True)
    own_attn = lax.all_gather(piece_attn, "dp", axis=0, tiled=True)
    owned = (
        jnp.concatenate([own_attn[:shard_rows], own_attn[shard_rows:, :qkv_tail]], axis=1),
        own_attn[shard_rows:, qkv_tail:],
        jnp.concatenate([own_expand[:shard_rows], own_expand[shard_rows:]], axis=1),
        own_down,
        small[:own_gains],
        small[own_gains:],
    )
    rates = (RATE_MATRIX, RATE_OUT, RATE_MATRIX, RATE_MATRIX, RATE_VECTOR, RATE_VECTOR)
    decays = (DECAY, DECAY, DECAY, DECAY, 0.0, 0.0)
    grads_low, updated, momenta, variances = ([], [], [], [])
    for master, first_old, second_old, gradient_low, step_rate, decay_rate in zip(
        masters, firsts, seconds, owned, rates, decays
    ):
        gradient = gradient_low.astype(jnp.float32)
        weight_new, first_new, second_new = adamw(
            master, first_old, second_old, gradient, step_rate, decay_rate
        )
        grads_low.append(gradient.astype(jnp.bfloat16))
        updated.append(weight_new)
        momenta.append(first_new)
        variances.append(second_new)
    return (
        output,
        token_grad,
        grads_low[0],
        grads_low[1],
        grads_low[2],
        grads_low[3],
        grads_low[4],
        grads_low[5],
        updated[0],
        updated[1],
        updated[2],
        updated[3],
        updated[4],
        updated[5],
        momenta[0],
        momenta[1],
        momenta[2],
        momenta[3],
        momenta[4],
        momenta[5],
        variances[0],
        variances[1],
        variances[2],
        variances[3],
        variances[4],
        variances[5],
    )


def solution(mesh):
    in_specs = (
        P(("dp", "group"), None),
        P(("dp", "group"), None),
        P(("dp", "group"), None),
        P("group", None),
        P("group", None),
        P("group", None),
        P("group", None),
        P("group"),
        P("group"),
        P("group", None),
        P("group", None),
        P("group", None),
        P("group", None),
        P("group"),
        P("group"),
        P("group", None),
        P("group", None),
        P("group", None),
        P("group", None),
        P("group"),
        P("group"),
    )
    out_specs = (
        P(("dp", "group"), None),
        P(("dp", "group"), None),
        P("group", None),
        P("group", None),
        P("group", None),
        P("group", None),
        P("group"),
        P("group"),
        P("group", None),
        P("group", None),
        P("group", None),
        P("group", None),
        P("group"),
        P("group"),
        P("group", None),
        P("group", None),
        P("group", None),
        P("group", None),
        P("group"),
        P("group"),
        P("group", None),
        P("group", None),
        P("group", None),
        P("group", None),
        P("group"),
        P("group"),
    )
    return jax.shard_map(local, mesh=mesh, in_specs=in_specs, out_specs=out_specs, check_vma=False)
```
